32 devices in a mesh: req: 8 (over z, y), hid: 4 (over x, core).
Axes of the slice: x: 2, y: 2, z: 4, core: 2. Of those that a mesh axis runs over, the one named last changes fastest.
Arguments:
- hidden_in: bfloat16 [8, 512, 1536], P('req', 'hid'), may hold values from -6 to 6
- queries: bfloat16 [8, 512, 1536], P('req', 'hid'), may hold values from -4 to 4
- cache_keys: bfloat16 [8, 4096, 256], P('req', 'hid'), may hold values from -6 to 6
- cache_values: bfloat16 [8, 4096, 256], P('req', 'hid'), may hold values from -6 to 6
- lengths: int32 [8], P('req'), may hold values from 256 to 4096, as said below
- routes: int32 [8, 512, 4], P('req'), may hold values from 0 to 7, all different within a row; in each aligned block of 128 rows (0 to 127, 128 to 255, ..., all dimensions but the last counted through in order) at most 128 rows name the same one
- attn_gain: float32 [1536], replicated, may hold values from 0.25 to 1.75
- key_proj: bfloat16 [1536, 256], replicated, may hold values from -0.15625 to 0.15625
- value_proj: bfloat16 [1536, 256], replicated, may hold values from -0.15625 to 0.15625
- out_proj: bfloat16 [1536, 1536], replicated, may hold values from -0.15625 to 0.15625
- moe_gain: float32 [1536], replicated, may hold values from 0.25 to 1.75
- router: bfloat16 [1536, 8], replicated, may hold values from -0.3125 to 0.3125
- gate_up: bfloat16 [8, 2, 1536, 768], P('req', None, None, 'hid'), may hold values from -0.15625 to 0.15625
- down_proj: bfloat16 [8, 768, 1536], P('req', 'hid'), may hold values from -0.21875 to 0.21875
Outputs:
- layer_out: bfloat16 [8, 512, 1536], P('req', 'hid')
- new_keys: bfloat16 [8, 512, 256], P('req', 'hid')
- new_values: bfloat16 [8, 512, 256], P('req', 'hid')
The draws below stay inside these ranges and needn't reach their ends.
Inputs may be any that keep to these rules, and one draw needn't show every extreme that they name: `routes`: each row names 4 different experts; within each aligned block of 128 tokens (the tokens of one device) no expert is named by more than 128 tokens, and in some block one expert is named by exactly 128. `lengths`: some request holds exactly 4096 cached positions and some other exactly 256.
All inputs are finite; a program needn't handle non-finite values.
Results may differ from the reference program's by a relative error of at most 0.015.
Values may be sent and summed in bfloat16 or wider, within the bound.
A program may use at most 128 MiB of HBM per device.

```python
import math
import jax
import jax.numpy as jnp
import numpy as np
from jax import lax

D = 1536
QH = 12
KVH = 2
HD = 128
FF = 768
TOP = 4
EXPERTS = 8
QW = 1536
KVW = 256
TOK_DEV = 128
SPAN = 512
CACHE = 4096
REQUESTS = 8
CAP = 128
N_HID = 4


def draw_queries(key, part):
    base_key = jax.random.fold_in(key, 11)
    values = jnp.clip(jax.random.normal(base_key, (REQUESTS, SPAN, QW), jnp.float32), -4.0, 4.0)
    return values.astype(jnp.bfloat16)


def draw_cache_keys(key, part):
    base_key = jax.random.fold_in(key, 23)
    values = jnp.clip(jax.random.normal(base_key, (REQUESTS, CACHE, KVW), jnp.float32), -6.0, 6.0)
    return values.astype(jnp.bfloat16)


def draw_lengths(key, part):
    drawn = jax.random.randint(jax.random.fold_in(key, 41), (REQUESTS,), CACHE // 16, CACHE + 1)
    longest = jax.random.randint(jax.random.fold_in(key, 43), (), 0, REQUESTS)
    other_step = jax.random.randint(jax.random.fold_in(key, 47), (), 1, REQUESTS)
    shortest = (longest + other_step) % REQUESTS
    drawn = drawn.at[longest].set(CACHE)
    drawn = drawn.at[shortest].set(CACHE // 16)
    return drawn.astype(jnp.int32)


def level_of(stream_key, extent, cuts, smallest, largest):
    gain = 1.0
    for axis_at, parts in cuts:
        steps = jax.random.uniform(jax.random.fold_in(jax.random.fold_in(stream_key, 6), axis_at), (parts,), jnp.float32, smallest / len(cuts), largest / len(cuts))
        gain = gain * jnp.repeat(jnp.exp(steps), extent[axis_at] // parts).reshape((-1,) + (1,) * (len(extent) - 1 - axis_at))
    return gain


def assign_block(stream_key, own, number, rows, number_of, top, most, slope):
    ranking = jax.random.permutation(stream_key, number_of)
    crowded, usual = shares(number_of, rows * top, most, slope, True), shares(number_of, rows * top, most, slope, False)
    places = jnp.arange(number_of)

    def named(sizes, offset_by):
        used = int((sizes > 0).sum())
        fixed = max(1, used // 4)
        moved = fixed + (places - fixed + offset_by * (used - fixed)) % max(1, number_of - fixed)
        return jnp.zeros((number_of,), jnp.int32).at[ranking[jnp.where(places < fixed, places, moved)]].set(jnp.asarray(sizes, jnp.int32))

    sizes = jnp.where(number % 4 == 0, named(crowded, number // 4), named(usual, number - number // 4 - 1))
    mixed = jax.random.permutation(jax.random.fold_in(own, 3), number_of)
    donor, sink = mixed[0:number_of // 2 * 2:2], mixed[1:number_of // 2 * 2:2]
    margin = jnp.minimum(sizes[donor] - 1, most - sizes[sink]) // 2
    margin = jnp.where((donor == ranking[0]) | (sink == ranking[0]) | (sizes[sink] == 0), 0, jnp.maximum(margin, 0))
    moved = jax.random.randint(jax.random.fold_in(own, 4), (number_of // 2,), 0, 1 << 20) % (margin + 1)
    sizes = sizes.at[donor].add(-moved).at[sink].add(moved)
    labels = jnp.searchsorted(jnp.cumsum(sizes), jnp.arange(rows * top), side="right").astype(jnp.int32)
    listing = labels.reshape(top, rows).T
    listing = listing[jax.random.permutation(jax.random.fold_in(own, 1), rows)]
    offset_by = jax.random.randint(jax.random.fold_in(own, 2), (rows, 1), 0, top)
    return jnp.take_along_axis(listing, (jnp.arange(top)[None, :] + offset_by) % top, axis=1)


def shares(count, total, limit, skew, full):
    weights = [(1 << 20) // math.isqrt(standing ** skew) + 1 for standing in range(1, count + 1)]
    largest = limit if full else min(limit, max(-(-total // count), total * weights[0] // sum(weights)))
    least = 1 if total - largest >= count - 1 else 0
    holding, surplus = [largest] + [least] * (count - 1), total - largest - least * (count - 1)
    while surplus > 0:
        free = [i for i in range(1, count) if holding[i] < largest] or [i for i in range(1, count) if holding[i] < limit]
        mass, remaining = sum([weights[i] for i in free]), surplus
        for i in free:
            extra = min(limit - holding[i], max(1, remaining * weights[i] // mass), surplus)
            holding[i] = holding[i] + extra
            surplus = surplus - extra
    return np.array(holding)


def bell_draw(stream_key, shape, scale, most, split=(), kind=jnp.bfloat16):
    entries = scale * jax.random.normal(stream_key, shape, jnp.float32)
    if split:
        entries = entries * level_of(stream_key, shape, split, -0.22, 0.18)
    return jnp.clip(entries, -most, most).astype(kind)


def setup_inputs(seed: int = 0) -> dict:
    splits = jax.random.split(jax.random.key(seed), 15)
    hidden_in = bell_draw(splits[0], (REQUESTS, SPAN, D), 1.0, 6.0, ((0, 8), (1, 4)))
    queries = draw_queries(jax.random.fold_in(splits[14], 71), 0)
    cache_keys = draw_cache_keys(jax.random.fold_in(splits[14], 71), 0)
    cache_values = bell_draw(splits[3], (REQUESTS, CACHE, KVW), 1.0, 6.0, ((0, 8), (1, 4)))
    lengths = draw_lengths(jax.random.fold_in(splits[14], 71), 0)
    routes_keys = jax.random.split(jax.random.fold_in(splits[5], 1), REQUESTS * SPAN // TOK_DEV)
    routes_turns = jax.random.permutation(jax.random.fold_in(splits[5], 3), REQUESTS * SPAN // TOK_DEV)
    routes = jax.vmap(lambda own, number: assign_block(jax.random.fold_in(splits[5], 2), own, number, TOK_DEV, EXPERTS, TOP, CAP, 2))(routes_keys, routes_turns).reshape((REQUESTS, SPAN, TOP))
    attn_gain = jnp.clip(1.0 + 0.15 * jax.random.normal(splits[6], (D,), jnp.float32), 0.25, 1.75)
    key_proj = bell_draw(splits[7], (D, KVW), D ** -0.5, 0.15625)
    value_proj = bell_draw(splits[8], (D, KVW), D ** -0.5, 0.15625)
    out_proj = bell_draw(splits[9], (QW, D), QW ** -0.5, 0.15625)
    moe_gain = jnp.clip(1.0 + 0.15 * jax.random.normal(splits[10], (D,), jnp.float32), 0.25, 1.75)
    router = bell_draw(splits[11], (D, EXPERTS), (D // 4) ** -0.5, 0.3125)
    gate_up = bell_draw(splits[12], (EXPERTS, 2, D, FF), D ** -0.5, 0.15625, ((0, 8), (3, 4)))
    down_proj = bell_draw(splits[13], (EXPERTS, FF, D), FF ** -0.5, 0.21875, ((0, 8), (1, 4)))
    return {"hidden_in": hidden_in, "queries": queries, "cache_keys": cache_keys, "cache_values": cache_values, "lengths": lengths, "routes": routes, "attn_gain": attn_gain, "key_proj": key_proj, "value_proj": value_proj, "out_proj": out_proj, "moe_gain": moe_gain, "router": router, "gate_up": gate_up, "down_proj": down_proj}


EPS = 1e-06
MASKED_SCORE = -1e+30

def normalize(row_data, gain_vector):
    row_data = row_data.astype(jnp.float32)
    return row_data * lax.rsqrt(lax.optimization_barrier(jnp.mean(row_data * row_data, axis=-1, keepdims=True)) + EPS) * gain_vector.astype(jnp.float32)

def attend(packed):
    queries, keys_old, values_old, keys_new, values_new, length = packed
    group_size = QH // KVH
    grouped = queries.astype(jnp.float32).reshape(SPAN, KVH, group_size, HD)
    key_rows = jnp.concatenate([keys_old, keys_new], axis=0).astype(jnp.float32).reshape(CACHE + SPAN, KVH, HD)
    value_rows = jnp.concatenate([values_old, values_new], axis=0).astype(jnp.float32).reshape(CACHE + SPAN, KVH, HD)
    scores = jnp.einsum('tgsd,kgd->gstk', grouped, key_rows) * HD ** (-0.5)
    positions = jnp.arange(CACHE + SPAN, dtype=jnp.int32)
    token_pos = jnp.arange(SPAN, dtype=jnp.int32)
    visible = jnp.where(positions[None, :] < CACHE, positions[None, :] < length, positions[None, :] - CACHE <= token_pos[:, None])
    scores = jnp.where(visible, scores, MASKED_SCORE)
    row_max = lax.optimization_barrier(jnp.max(scores, axis=-1, keepdims=True))
    weights = jnp.where(visible, jnp.exp(scores - row_max), 0.0)
    totals = lax.optimization_barrier(jnp.sum(weights, axis=-1))
    probs = lax.optimization_barrier(weights.astype(jnp.bfloat16))
    mixture = jnp.einsum('gstk,kgd->tgsd', probs.astype(jnp.float32), value_rows)
    mixture = mixture / jnp.transpose(totals, (2, 0, 1))[..., None]
    return mixture.reshape(SPAN, QW).astype(jnp.bfloat16)

def reference(hidden_in, queries, cache_keys, cache_values, lengths, routes, attn_gain, key_proj, value_proj, out_proj, moe_gain, router, gate_up, down_proj):
    flat_in = hidden_in.reshape(REQUESTS * SPAN, D)
    normed = normalize(flat_in, attn_gain).astype(jnp.bfloat16)
    new_keys = jnp.dot(normed, key_proj, preferred_element_type=jnp.float32).astype(jnp.bfloat16).reshape(REQUESTS, SPAN, KVW)
    new_values = jnp.dot(normed, value_proj, preferred_element_type=jnp.float32).astype(jnp.bfloat16).reshape(REQUESTS, SPAN, KVW)
    attended = lax.map(attend, (queries, cache_keys, cache_values, new_keys, new_values, lengths))
    mid_stream = (flat_in.astype(jnp.float32) + jnp.dot(attended.reshape(REQUESTS * SPAN, QW), out_proj, preferred_element_type=jnp.float32)).astype(jnp.bfloat16)
    moe_in = normalize(mid_stream, moe_gain).astype(jnp.bfloat16)
    logits = jnp.dot(moe_in, router, preferred_element_type=jnp.float32)
    chosen = routes.reshape(REQUESTS * SPAN, TOP).astype(jnp.int32)
    picked = jnp.take_along_axis(logits, chosen, axis=1)
    gate_values = jax.nn.sigmoid(picked)
    weights = gate_values / lax.optimization_barrier(jnp.sum(gate_values, axis=1, keepdims=True))
    block_count = REQUESTS * SPAN // TOK_DEV
    pair_count = TOK_DEV * TOP
    blocks = chosen.reshape(block_count, pair_count)
    onehot = (blocks[..., None] == jnp.arange(EXPERTS, dtype=jnp.int32)).astype(jnp.int32)
    slot_ids = lax.optimization_barrier(jnp.sum((jnp.cumsum(onehot, axis=1) - 1) * onehot, axis=-1)).astype(jnp.int32)
    block_ids = jnp.arange(block_count, dtype=jnp.int32)[:, None]
    pair_token = jnp.broadcast_to((jnp.arange(pair_count, dtype=jnp.int32) // TOP)[None, :], (block_count, pair_count))
    slot_table = jnp.full((block_count, EXPERTS, CAP), TOK_DEV, jnp.int32)
    slot_table = slot_table.at[block_ids, blocks, slot_ids].set(pair_token)
    padded = jnp.concatenate([moe_in.reshape(block_count, TOK_DEV, D), jnp.zeros((block_count, 1, D), jnp.bfloat16)], axis=1)
    slice_width = FF // N_HID

    def run_expert(packed):
        indices, gate_weights, down_weights = packed
        row_data = padded[block_ids, indices].reshape(block_count * CAP, D)
        gate_out = jnp.dot(row_data, gate_weights[0], preferred_element_type=jnp.float32)
        up_out = jnp.dot(row_data, gate_weights[1], preferred_element_type=jnp.float32)
        activation = (jnp.maximum(gate_out, 0.0) * up_out).astype(jnp.bfloat16)
        partials = jnp.stack([jnp.dot(activation[:, portion * slice_width:(portion + 1) * slice_width], down_weights[portion * slice_width:(portion + 1) * slice_width], preferred_element_type=jnp.float32).astype(jnp.bfloat16) for portion in range(N_HID)])
        partials = lax.optimization_barrier(partials)
        return lax.optimization_barrier(jnp.sum(partials.astype(jnp.float32), axis=0)).astype(jnp.bfloat16).reshape(block_count, CAP, D)
    results = lax.map(run_expert, (jnp.transpose(slot_table, (1, 0, 2)), gate_up, down_proj))
    fetched = results[blocks, block_ids, slot_ids].reshape(REQUESTS * SPAN, TOP, D).astype(jnp.float32)
    moe_out = lax.optimization_barrier(jnp.sum(weights[..., None] * fetched, axis=1))
    layer_out = (mid_stream.astype(jnp.float32) + moe_out).astype(jnp.bfloat16).reshape(REQUESTS, SPAN, D)
    return (layer_out, new_keys, new_values)
```

```python
import functools

import jax
import jax.numpy as jnp
from jax import lax
from jax.experimental import pallas as pl
from jax.experimental.pallas import tpu as pltpu
from jax.sharding import PartitionSpec as P

QH = 12
KVH = 2
HD = 128
GROUP = QH // KVH
EPS = 1e-06
MASKED_SCORE = -1e30
EXP2_SCALE = HD ** (-0.5) * 1.4426950408889634
ROW_TILE = 256
MESH = pl.DeviceIdType.MESH


def normalize(row_data, gain_vector):
    row_data = row_data.astype(jnp.float32)
    return (
        row_data
        * lax.rsqrt(jnp.mean(row_data * row_data, axis=-1, keepdims=True) + EPS)
        * gain_vector
    )


def dot_nt(left, right):
    return lax.dot_general(
        left, right, (((1,), (1,)), ((), ())), preferred_element_type=jnp.float32
    )


def layer_kernel(
    steps,
    hidden,
    queries,
    cache_keys,
    cache_values,
    lengths,
    routes_t,
    attn_gain,
    key_proj,
    value_proj,
    out_proj,
    moe_gain,
    router_t,
    gate_up,
    down_proj,
    layer_out,
    new_keys,
    new_values,
    kv,
    heads,
    acc,
    row_max,
    attended,
    out_w,
    mid,
    gate_in,
    gates,
    downs,
    act,
    toks,
    wts,
    parts,
    part_in,
    sum_in,
    local_sem,
    hid_send,
    hid_recv,
    req_send,
    req_recv,
):
    own = hidden.shape[0]
    half = cache_keys.shape[0] // 2
    span_slot = kv.shape[0] - 1
    width = gate_up.shape[2]
    experts = router_t.shape[0]
    me = lax.axis_index("hid")
    pair = me + 1 - 2 * lax.rem(me, 2)
    across = lax.rem(me + 2, 4)
    corner = 3 - me
    row = lax.axis_index("req")
    line, side = row // 2, lax.rem(row, 2)
    twin = {"req": line * 2 + 1 - side}

    def along(step):
        return {"req": lax.rem(line + step, steps) * 2 + side}

    barrier = pltpu.get_barrier_semaphore()
    for peer in [{"hid": pair}, {"hid": across}, twin] + [along(d) for d in range(1, steps)]:
        pl.semaphore_signal(barrier, inc=1, device_id=peer, device_id_type=MESH)
    pl.semaphore_wait(barrier, steps + 2)

    def hid_copy(src, dst, number, peer):
        return pltpu.make_async_remote_copy(
            src_ref=src,
            dst_ref=dst,
            send_sem=hid_send.at[number],
            recv_sem=hid_recv.at[number],
            device_id={"hid": peer},
            device_id_type=MESH,
        )

    def req_copy(src, dst, kind, slot, peer):
        return pltpu.make_async_remote_copy(
            src_ref=src,
            dst_ref=dst,
            send_sem=req_send.at[kind, slot],
            recv_sem=req_recv.at[kind, slot],
            device_id=peer,
            device_id_type=MESH,
        )

    cached = [
        (ref.at[pl.ds(part * half, half)], part, which)
        for part in range(2)
        for which, ref in enumerate((cache_keys, cache_values))
    ]
    for n, (src, part, which) in enumerate(cached):
        hid_copy(src, kv.at[me * 2 + part, which], n, across).start()
    for n, (src, part, which) in enumerate(cached):
        hid_copy(src, kv.at[me * 2 + part, which], 4 + n, pair).start()

    def own_block(n):
        src, part, which = cached[n]
        return pltpu.make_async_copy(src, kv.at[me * 2 + part, which], local_sem.at[n])

    for n in range(4):
        own_block(n).start()
    gate_load = pltpu.make_async_copy(gate_up, gate_in, local_sem.at[4])
    gate_load.start()
    down_load = pltpu.make_async_copy(down_proj, downs.at[me], local_sem.at[5])
    down_load.start()
    out_load = pltpu.make_async_copy(out_proj, out_w, local_sem.at[6])
    out_load.start()

    normed = normalize(hidden[...], attn_gain[...]).astype(jnp.bfloat16)
    own_rows = pl.ds(pl.multiple_of(me * own, own), own)
    for which, (proj, dest) in enumerate(((key_proj, new_keys), (value_proj, new_values))):
        fresh = jnp.dot(normed, proj[...], preferred_element_type=jnp.float32).astype(jnp.bfloat16)
        dest[...] = fresh
        kv[span_slot, which, own_rows, :] = fresh

    def span_rows(which, owner):
        return kv.at[span_slot, which, pl.ds(pl.multiple_of(owner * own, own), own)]

    for which in range(2):
        hid_copy(span_rows(which, me), span_rows(which, me), 12 + which, across).start()
        hid_copy(span_rows(which, me), span_rows(which, me), 14 + which, pair).start()

    for g in range(KVH):
        for i in range(GROUP):
            heads[g, i * own : (i + 1) * own, :] = queries[
                :, (g * GROUP + i) * HD : (g * GROUP + i + 1) * HD
            ]
    acc[...] = jnp.zeros_like(acc)
    row_max[...] = jnp.full_like(row_max, MASKED_SCORE)

    gate_load.wait()
    gates[me, :, 0:width] = gate_in[0]
    gates[me, :, width : 2 * width] = gate_in[1]
    hid_copy(gates.at[me], gates.at[me], 20, pair).start()
    hid_copy(down_proj, downs.at[me], 21, pair).start()

    def landed(dst, number):
        hid_copy(dst, dst, number, pair).wait_recv()

    length = lengths[0]
    ones = jnp.ones((half, HD), jnp.bfloat16)

    def step_body(step, carry):
        for n in range(2):

            @pl.when(step == n)
            def _():
                own_block(2 * n).wait()
                own_block(2 * n + 1).wait()

            @pl.when(step == 2 + n)
            def _():
                for which in range(2):
                    landed(kv.at[pair * 2 + n, which], 4 + 2 * n + which)

            @pl.when(step == 5 + 2 * n)
            def _():
                for which in range(2):
                    block = kv.at[across * 2 + n, which]
                    landed(block, 2 * n + which)
                    hid_copy(block, block, 8 + 2 * n + which, pair).start()
                if n == 1:
                    hid_copy(gates.at[me], gates.at[me], 18, across).start()
                    hid_copy(down_proj, downs.at[me], 19, across).start()

            @pl.when(step == 6 + 2 * n)
            def _():
                for which in range(2):
                    landed(kv.at[corner * 2 + n, which], 8 + 2 * n + which)

        @pl.when(step == 4)
        def _():
            for which in range(2):
                block = span_rows(which, across)
                landed(block, 12 + which)
                hid_copy(block, block, 16 + which, pair).start()
            for which in range(2):
                landed(span_rows(which, pair), 14 + which)
                landed(span_rows(which, corner), 16 + which)

        late = (step + 3) // 8
        span = (step + 4) // 8 - late
        early = 1 - span - late
        slot = (
            early * (2 * (me + (step // 2) * (pair - me)) + lax.rem(step, 2))
            + span * span_slot
            + late * (2 * (across + lax.rem(step + 1, 2) * (corner - across)) + (step + 1) // 2 - 3)
        )
        token = lax.broadcasted_iota(jnp.int32, (ROW_TILE, half), 0) % own
        column = lax.broadcasted_iota(jnp.int32, (ROW_TILE, half), 1)
        limit = (1 - span) * (length - slot * half) + span * (me * own + 1)
        visible = column < limit + span * token
        for g in range(KVH):
            keys = kv[slot, 0, :, g * HD : (g + 1) * HD]
            values = jnp.concatenate([kv[slot, 1, :, g * HD : (g + 1) * HD], ones], axis=1)
            for tile in range(GROUP * own // ROW_TILE):
                rows = slice(tile * ROW_TILE, (tile + 1) * ROW_TILE)
                scores = jnp.where(visible, dot_nt(heads[g, rows, :], keys), MASKED_SCORE)
                old_max = row_max[g, rows, :]
                new_max = jnp.maximum(old_max, jnp.max(scores, axis=1, keepdims=True))
                row_max[g, rows, :] = new_max
                rescale = jnp.exp2((old_max - new_max) * EXP2_SCALE)
                shift = jnp.concatenate([new_max] * (half // HD), axis=1)
                probs = jnp.exp2((scores - shift) * EXP2_SCALE).astype(jnp.bfloat16)
                acc[g, rows, :] = acc[g, rows, :] * jnp.concatenate([rescale, rescale], axis=1) + (
                    jnp.dot(probs, values, preferred_element_type=jnp.float32)
                )
        return carry

    lax.fori_loop(0, 9, step_body, 0)

    for g in range(KVH):
        for i in range(GROUP):
            rows = slice(i * own, (i + 1) * own)
            head = g * GROUP + i
            attended[:, head * HD : (head + 1) * HD] = (
                acc[g, rows, 0:HD] / acc[g, rows, HD : 2 * HD]
            ).astype(jnp.bfloat16)
    out_load.wait()
    cols = 512
    model = hidden.shape[1]
    for c in range(model // cols):
        at = slice(c * cols, (c + 1) * cols)
        mid[:, at] = (
            hidden[:, at].astype(jnp.float32)
            + jnp.dot(attended[...], out_w[:, at], preferred_element_type=jnp.float32)
        ).astype(jnp.bfloat16)

    moe_in = normalize(mid[...], moe_gain[...]).astype(jnp.bfloat16)
    toks[line, side] = moe_in
    logits = dot_nt(router_t[...], moe_in)
    own_routes = routes_t[:, own_rows]
    expert_ids = lax.broadcasted_iota(jnp.int32, (experts, own), 0)
    chosen = expert_ids == own_routes[0:1, :]
    for k in range(1, own_routes.shape[0]):
        chosen = chosen | (expert_ids == own_routes[k : k + 1, :])
    gate_values = jnp.where(chosen, jax.nn.sigmoid(logits), 0.0)
    weights = gate_values / jnp.sum(gate_values, axis=0, keepdims=True)
    high = weights.astype(jnp.bfloat16).astype(jnp.float32)
    wts[line, side] = jnp.concatenate([high, weights - high], axis=0).astype(jnp.bfloat16)

    def at_step(d):
        return lax.rem(line + steps - d, steps)

    for n, ref in enumerate((toks, wts)):
        req_copy(ref.at[line, side], ref.at[line, side], n, 0, twin).start()
        for d in range(1, steps):
            req_copy(ref.at[line, side], ref.at[line, side], 2 + n, d, along(d)).start()

    def pass_on(d, carry):
        for n, ref in enumerate((toks, wts)):
            block = ref.at[at_step(d), side]
            req_copy(block, block, 2 + n, d, twin).wait_recv()
            req_copy(block, block, n, d, twin).start()
        return carry

    lax.fori_loop(1, steps, pass_on, 0)

    down_load.wait()
    for n, ref in enumerate((gates, downs)):
        landed(ref.at[across], 18 + n)
        hid_copy(ref.at[across], ref.at[across], 22 + n, pair).start()
    for n, ref in enumerate((gates, downs)):
        landed(ref.at[pair], 20 + n)
        landed(ref.at[corner], 22 + n)

    pick = (lax.broadcasted_iota(jnp.int32, (2 * experts, HD), 0) % experts == row).astype(
        jnp.bfloat16
    )

    def expert_step(e, carry):
        d = lax.rem(e + 1, steps)
        source = at_step(d)
        for n, ref in enumerate((toks, wts)):
            block = ref.at[source, 1 - side]
            req_copy(block, block, n, d, twin).wait_recv()
        rows = toks[source].reshape(2 * own, model)
        for h in range(4):
            both = jnp.dot(rows, gates[h], preferred_element_type=jnp.float32)
            act[:, h * width : (h + 1) * width] = (
                jnp.maximum(both[:, 0:width], 0.0) * both[:, width : 2 * width]
            ).astype(jnp.bfloat16)
        share = jnp.concatenate(
            [
                lax.dot_general(
                    wts[source, s],
                    pick,
                    (((0,), (0,)), ((), ())),
                    preferred_element_type=jnp.float32,
                )
                for s in range(2)
            ],
            axis=0,
        )
        share = jnp.concatenate([share] * (cols // HD), axis=1)
        for c in range(model // cols):
            at = slice(c * cols, (c + 1) * cols)
            block = jnp.dot(
                act[...],
                downs[:, :, at].reshape(4 * width, cols),
                preferred_element_type=jnp.float32,
            )
            parts[d, :, :, at] = (block * share).astype(jnp.bfloat16).reshape(2, own, cols)
        req_copy(parts.at[d, 1 - side], part_in.at[d], 4, d, twin).start()

        @pl.when(e >= 1)
        def _():
            req_copy(part_in.at[e], part_in.at[e], 4, e, twin).wait_recv()
            parts[e, side] = (
                parts[e, side].astype(jnp.float32) + part_in[e].astype(jnp.float32)
            ).astype(jnp.bfloat16)
            req_copy(
                parts.at[e, side],
                sum_in.at[e - 1],
                5,
                e,
                {"req": at_step(e) * 2 + side},
            ).start()

        return carry

    lax.fori_loop(0, steps, expert_step, 0)

    total = mid[...].astype(jnp.float32) + parts[0, side].astype(jnp.float32)
    for d in range(1, steps):
        req_copy(sum_in.at[d - 1], sum_in.at[d - 1], 5, d, twin).wait_recv()
        total = total + sum_in[d - 1].astype(jnp.float32)
    req_copy(part_in.at[0], part_in.at[0], 4, 0, twin).wait_recv()
    layer_out[...] = (total + part_in[0].astype(jnp.float32)).astype(jnp.bfloat16)

    for n in range(12):
        src, part, which = cached[n % 4]
        hid_copy(src, kv.at[me * 2 + part, which], n, pair).wait_send()
    for n in range(12, 18):
        hid_copy(span_rows(0, me), span_rows(0, me), n, pair).wait_send()
    for n in range(18, 24):
        ref = (gates, downs)[n % 2]
        hid_copy(ref.at[me], ref.at[me], n, pair).wait_send()
    for n, ref in enumerate((toks, wts)):
        for d in range(steps):
            req_copy(ref.at[line, side], ref.at[line, side], n, d, twin).wait_send()
            if d:
                req_copy(ref.at[line, side], ref.at[line, side], 2 + n, d, twin).wait_send()
    for d in range(steps):
        req_copy(part_in.at[d], part_in.at[d], 4, d, twin).wait_send()
        if d:
            req_copy(parts.at[d, side], parts.at[d, side], 5, d, twin).wait_send()


def body(
    hidden_in,
    queries,
    cache_keys,
    cache_values,
    lengths,
    routes,
    attn_gain,
    key_proj,
    value_proj,
    out_proj,
    moe_gain,
    router,
    gate_up,
    down_proj,
):
    own, model = hidden_in.shape[1:]
    kv_width = key_proj.shape[1]
    cached = cache_keys.shape[1]
    steps = lax.axis_size("req") // 2
    experts = router.shape[1]
    width = gate_up.shape[3]
    bf16 = jnp.bfloat16
    vmem = pl.BlockSpec(memory_space=pltpu.VMEM)
    smem = pl.BlockSpec(memory_space=pltpu.SMEM)
    anywhere = pl.BlockSpec(memory_space=pl.ANY)
    layer_out, new_keys, new_values = pl.pallas_call(
        functools.partial(layer_kernel, steps),
        out_shape=(
            jax.ShapeDtypeStruct((own, model), bf16),
            jax.ShapeDtypeStruct((own, kv_width), bf16),
            jax.ShapeDtypeStruct((own, kv_width), bf16),
        ),
        in_specs=[
            vmem,
            vmem,
            anywhere,
            anywhere,
            smem,
            vmem,
            vmem,
            vmem,
            vmem,
            anywhere,
            vmem,
            vmem,
            anywhere,
            anywhere,
        ],
        out_specs=(vmem, vmem, vmem),
        scratch_shapes=[
            pltpu.VMEM((9, 2, cached // 2, kv_width), bf16),
            pltpu.VMEM((KVH, GROUP * own, HD), bf16),
            pltpu.VMEM((KVH, GROUP * own, 2 * HD), jnp.float32),
            pltpu.VMEM((KVH, GROUP * own, HD), jnp.float32),
            pltpu.VMEM((own, QH * HD), bf16),
            pltpu.VMEM(out_proj.shape, bf16),
            pltpu.VMEM((own, model), bf16),
            pltpu.VMEM((2, model, width), bf16),
            pltpu.VMEM((4, model, 2 * width), bf16),
            pltpu.VMEM((4, width, model), bf16),
            pltpu.VMEM((2 * own, 4 * width), bf16),
            pltpu.VMEM((steps, 2, own, model), bf16),
            pltpu.VMEM((steps, 2, 2 * experts, own), bf16),
            pltpu.VMEM((steps, 2, own, model), bf16),
            pltpu.VMEM((steps, own, model), bf16),
            pltpu.VMEM((steps - 1, own, model), bf16),
            pltpu.SemaphoreType.DMA((7,)),
            pltpu.SemaphoreType.DMA((24,)),
            pltpu.SemaphoreType.DMA((24,)),
            pltpu.SemaphoreType.DMA((6, steps)),
            pltpu.SemaphoreType.DMA((6, steps)),
        ],
        compiler_params=pltpu.CompilerParams(
            collective_id=0, has_side_effects=True, vmem_limit_bytes=VMEM_LIMIT
        ),
    )(
        hidden_in[0],
        queries[0],
        cache_keys[0],
        cache_values[0],
        lengths,
        routes[0].T,
        attn_gain[None],
        key_proj,
        value_proj,
        out_proj,
        moe_gain[None],
        router.T,
        gate_up[0],
        down_proj[0],
    )
    return (layer_out[None], new_keys[None], new_values[None])


VMEM_LIMIT = 64 * 1024 * 1024 - 512 * 1024


def solution(mesh):
    in_specs = (
        P("req", "hid", None),
        P("req", "hid", None),
        P("req", "hid", None),
        P("req", "hid", None),
        P("req"),
        P("req", None, None),
        P(),
        P(),
        P(),
        P(),
        P(),
        P(),
        P("req", None, None, "hid"),
        P("req", "hid", None),
    )
    out_specs = (P("req", "hid", None), P("req", "hid", None), P("req", "hid", None))
    return jax.shard_map(body, mesh=mesh, in_specs=in_specs, out_specs=out_specs, check_vma=False)
```

```python
import functools

import jax
import jax.numpy as jnp
from jax import lax
from jax.experimental import pallas as pl
from jax.experimental.pallas import tpu as pltpu
from jax.sharding import PartitionSpec as P

QH = 12
KVH = 2
HD = 128
GROUP = QH // KVH
EPS = 1e-06
MASKED_SCORE = -1e30
EXP2_SCALE = HD ** (-0.5) * 1.4426950408889634
ROW_TILE = 256
MESH = pl.DeviceIdType.MESH


def normalize(row_data, gain_vector):
    row_data = row_data.astype(jnp.float32)
    return (
        row_data
        * lax.rsqrt(jnp.mean(row_data * row_data, axis=-1, keepdims=True) + EPS)
        * gain_vector
    )


def dot_nt(left, right):
    return lax.dot_general(
        left, right, (((1,), (1,)), ((), ())), preferred_element_type=jnp.float32
    )


def layer_kernel(
    steps,
    hidden,
    queries,
    cache_keys,
    cache_values,
    lengths,
    routes_t,
    attn_gain,
    key_proj,
    value_proj,
    out_proj,
    moe_gain,
    router_t,
    gate_up,
    down_proj,
    layer_out,
    new_keys,
    new_values,
    kv,
    heads,
    acc,
    row_max,
    attended,
    out_w,
    mid,
    gates,
    downs,
    act,
    toks,
    wts,
    parts,
    part_in,
    sum_in,
    local_sem,
    hid_send,
    hid_recv,
    req_send,
    req_recv,
):
    own = hidden.shape[0]
    half = cache_keys.shape[0] // 2
    span_slot = kv.shape[0] - 1
    width = down_proj.shape[0]
    experts = router_t.shape[0]
    me = lax.axis_index("hid")
    pair = me + 1 - 2 * lax.rem(me, 2)
    across = lax.rem(me + 2, 4)
    corner = 3 - me
    row = lax.axis_index("req")
    line, side = row // 2, lax.rem(row, 2)
    core, column_of = lax.rem(me, 2), me // 2
    own_slot, pair_slot = side * 2 + core, side * 2 + 1 - core
    far_slot, corner_slot = (1 - side) * 2 + core, (1 - side) * 2 + 1 - core
    neighbour = {"req": line * 2 + 1 - side}
    twin = {"hid": across}

    def along(place):
        return {"req": place * 2 + side}

    barrier = pltpu.get_barrier_semaphore()
    others = [along(lax.rem(line + d, steps)) for d in range(1, steps)]
    for peer in [{"hid": pair}, twin, neighbour] + others:
        pl.semaphore_signal(barrier, inc=1, device_id=peer, device_id_type=MESH)
    pl.semaphore_wait(barrier, steps + 2)

    def hid_copy(src, dst, number, peer):
        peer = peer if isinstance(peer, dict) else {"hid": peer}
        return pltpu.make_async_remote_copy(
            src_ref=src,
            dst_ref=dst,
            send_sem=hid_send.at[number],
            recv_sem=hid_recv.at[number],
            device_id=peer,
            device_id_type=MESH,
        )

    def req_copy(src, dst, kind, slot, peer, landing=None):
        return pltpu.make_async_remote_copy(
            src_ref=src,
            dst_ref=dst,
            send_sem=req_send.at[kind, slot],
            recv_sem=req_recv.at[kind, slot if landing is None else landing],
            device_id=peer,
            device_id_type=MESH,
        )

    cached = [
        (ref.at[pl.ds(part * half, half)], part, which)
        for part in range(2)
        for which, ref in enumerate((cache_keys, cache_values))
    ]
    for n, (src, part, which) in enumerate(cached[:2]):
        hid_copy(src, kv.at[me * 2 + part, which], n, across).start()
    for n, (src, part, which) in enumerate(cached):
        hid_copy(src, kv.at[me * 2 + part, which], 4 + n, pair).start()

    def own_block(n):
        src, part, which = cached[n]
        return pltpu.make_async_copy(src, kv.at[me * 2 + part, which], local_sem.at[n])

    for n in range(4):
        own_block(n).start()
    for n, peer in ((18, neighbour), (20, pair)):
        hid_copy(gate_up, gates.at[own_slot], n, peer).start()
        hid_copy(down_proj, downs.at[own_slot], n + 1, peer).start()
    gate_load = pltpu.make_async_copy(gate_up, gates.at[own_slot], local_sem.at[4])
    gate_load.start()
    down_load = pltpu.make_async_copy(down_proj, downs.at[own_slot], local_sem.at[5])
    down_load.start()
    out_load = pltpu.make_async_copy(out_proj, out_w, local_sem.at[6])
    out_load.start()

    normed = normalize(hidden[...], attn_gain[...]).astype(jnp.bfloat16)
    own_rows = pl.ds(pl.multiple_of(me * own, own), own)
    for which, (proj, dest) in enumerate(((key_proj, new_keys), (value_proj, new_values))):
        fresh = jnp.dot(normed, proj[...], preferred_element_type=jnp.float32).astype(jnp.bfloat16)
        dest[...] = fresh
        kv[span_slot, which, own_rows, :] = fresh

    def span_rows(which, owner):
        return kv.at[span_slot, which, pl.ds(pl.multiple_of(owner * own, own), own)]

    for which in range(2):
        hid_copy(span_rows(which, me), span_rows(which, me), 12 + which, across).start()
        hid_copy(span_rows(which, me), span_rows(which, me), 14 + which, pair).start()
    for n, (src, part, which) in enumerate(cached[2:]):
        hid_copy(src, kv.at[me * 2 + part, which], 2 + n, across).start()

    for g in range(KVH):
        for i in range(GROUP):
            heads[g, i * own : (i + 1) * own, :] = queries[
                :, (g * GROUP + i) * HD : (g * GROUP + i + 1) * HD
            ]
    acc[...] = jnp.zeros_like(acc)
    row_max[...] = jnp.full_like(row_max, MASKED_SCORE)

    def landed(dst, number):
        hid_copy(dst, dst, number, pair).wait_recv()

    length = lengths[0]
    ones = jnp.ones((half, HD), jnp.bfloat16)

    def absorb(slot, hide):
        for g in range(KVH):
            keys = kv[slot, 0, :, g * HD : (g + 1) * HD]
            values = jnp.concatenate([kv[slot, 1, :, g * HD : (g + 1) * HD], ones], axis=1)
            for tile in range(GROUP * own // ROW_TILE):
                rows = slice(tile * ROW_TILE, (tile + 1) * ROW_TILE)
                scores = hide(dot_nt(heads[g, rows, :], keys))
                old_max = row_max[g, rows, :]
                new_max = jnp.maximum(old_max, jnp.max(scores, axis=1, keepdims=True))
                row_max[g, rows, :] = new_max
                rescale = jnp.exp2((old_max - new_max) * EXP2_SCALE)
                shift = jnp.concatenate([new_max] * (half // HD), axis=1)
                probs = jnp.exp2((scores - shift) * EXP2_SCALE).astype(jnp.bfloat16)
                acc[g, rows, :] = acc[g, rows, :] * jnp.concatenate([rescale, rescale], axis=1) + (
                    jnp.dot(probs, values, preferred_element_type=jnp.float32)
                )

    def step_body(step, carry):
        for n in range(2):

            @pl.when(step == n)
            def _():
                own_block(2 * n).wait()
                own_block(2 * n + 1).wait()

            @pl.when(step == 2 + n)
            def _():
                for which in range(2):
                    landed(kv.at[pair * 2 + n, which], 4 + 2 * n + which)

            @pl.when(step == 4 + 3 * n)
            def _():
                for which in range(2):
                    block = kv.at[across * 2 + n, which]
                    landed(block, 2 * n + which)
                    hid_copy(block, block, 8 + 2 * n + which, pair).start()

            @pl.when(step == 5 + 3 * n)
            def _():
                for which in range(2):
                    landed(kv.at[corner * 2 + n, which], 8 + 2 * n + which)

        @pl.when(step == 6)
        def _():
            for which in range(2):
                block = span_rows(which, across)
                landed(block, 12 + which)
                hid_copy(block, block, 16 + which, pair).start()
            for which in range(2):
                landed(span_rows(which, pair), 14 + which)
                landed(span_rows(which, corner), 16 + which)

        early = 1 - (step + 4) // 8
        part = (step + 1) // 8
        span = (step + 2) // 8 - part
        late = 1 - early - span
        slot = (
            early * (2 * (me + (step // 2) * (pair - me)) + lax.rem(step, 2))
            + span * span_slot
            + late * (2 * (across + lax.rem(step + part, 2) * (corner - across)) + part)
        )

        @pl.when(step != 6)
        def _():
            column = lax.broadcasted_iota(jnp.int32, (1, half), 1)
            bias = jnp.where(column < length - slot * half, 0.0, MASKED_SCORE)
            absorb(slot, lambda scores: scores + bias)

        @pl.when(step == 6)
        def _():
            token = lax.broadcasted_iota(jnp.int32, (ROW_TILE, half), 0) % own
            column = lax.broadcasted_iota(jnp.int32, (ROW_TILE, half), 1)
            visible = column <= me * own + token
            absorb(span_slot, lambda scores: jnp.where(visible, scores, MASKED_SCORE))

        return carry

    lax.fori_loop(0, 9, step_body, 0)

    for g in range(KVH):
        for i in range(GROUP):
            rows = slice(i * own, (i + 1) * own)
            head = g * GROUP + i
            attended[:, head * HD : (head + 1) * HD] = (
                acc[g, rows, 0:HD] / acc[g, rows, HD : 2 * HD]
            ).astype(jnp.bfloat16)
    out_load.wait()
    cols = 512
    model = hidden.shape[1]
    for c in range(model // cols):
        at = slice(c * cols, (c + 1) * cols)
        mid[:, at] = (
            hidden[:, at].astype(jnp.float32)
            + jnp.dot(attended[...], out_w[:, at], preferred_element_type=jnp.float32)
        ).astype(jnp.bfloat16)

    moe_in = normalize(mid[...], moe_gain[...]).astype(jnp.bfloat16)
    toks[line, column_of] = moe_in
    logits = dot_nt(router_t[...], moe_in)
    own_routes = routes_t[:, own_rows]
    expert_ids = lax.broadcasted_iota(jnp.int32, (experts, own), 0)
    chosen = expert_ids == own_routes[0:1, :]
    for k in range(1, own_routes.shape[0]):
        chosen = chosen | (expert_ids == own_routes[k : k + 1, :])
    gate_values = jnp.where(chosen, jax.nn.sigmoid(logits), 0.0)
    weights = gate_values / jnp.sum(gate_values, axis=0, keepdims=True)
    high = weights.astype(jnp.bfloat16).astype(jnp.float32)
    wts[line, column_of] = jnp.concatenate([high, weights - high], axis=0).astype(jnp.bfloat16)

    def toks_copy(n, place, kind, peer, slot):
        block = (toks, wts)[n].at[place, column_of]
        return req_copy(block, block, 2 * kind + n, slot, peer)

    def give(place, up, down):
        for n in range(2):

            @pl.when(up)
            def _():
                toks_copy(n, place, 1, along(line + 1), place).start()

            @pl.when(down)
            def _():
                toks_copy(n, place, 2, along(line - 1), place).start()

            toks_copy(n, place, 0, twin, place).start()

    def schedule(t):
        dist = lax.rem(t // 2 + 1, steps)
        up = lax.rem(t, 2)
        place = line - dist + 2 * dist * up
        return place, up, (place >= 0) & (place < steps) & (t < 2 * steps - 1)

    def pass_on(t):
        place, up, valid = schedule(t)
        valid = valid & (t < 2 * steps - 2)
        for n in range(2):

            @pl.when(valid & (up == 0))
            def _():
                toks_copy(n, place, 1, twin, place).wait_recv()

                @pl.when(line + 1 < steps)
                def _():
                    toks_copy(n, place, 1, along(line + 1), place).start()

            @pl.when(valid & (up == 1))
            def _():
                toks_copy(n, place, 2, twin, place).wait_recv()

                @pl.when(line >= 1)
                def _():
                    toks_copy(n, place, 2, along(line - 1), place).start()

            @pl.when(valid)
            def _():
                toks_copy(n, place, 0, twin, place).start()

    give(line, line + 1 < steps, line >= 1)

    pass_on(0)
    pass_on(1)

    gate_load.wait()
    down_load.wait()
    for n, ref in enumerate((gates, downs)):
        landed(ref.at[far_slot], 18 + n)
        hid_copy(ref.at[far_slot], ref.at[far_slot], 22 + n, pair).start()
    for n, ref in enumerate((gates, downs)):
        landed(ref.at[pair_slot], 20 + n)
        landed(ref.at[corner_slot], 22 + n)

    lane_half = lax.broadcasted_iota(jnp.int32, (2 * experts, 2 * HD), 1) // HD
    pick = (
        lax.broadcasted_iota(jnp.int32, (2 * experts, 2 * HD), 0) % experts == line * 2 + lane_half
    ).astype(jnp.bfloat16)

    def expert_rows(place):
        for n, ref in enumerate((toks, wts)):
            block = ref.at[place, 1 - column_of]
            req_copy(block, block, n, place, twin).wait_recv()
        rows = toks[place].reshape(2 * own, model)
        share = jnp.concatenate(
            [
                lax.dot_general(
                    wts[place, s],
                    pick,
                    (((0,), (0,)), ((), ())),
                    preferred_element_type=jnp.float32,
                )
                for s in range(2)
            ],
            axis=0,
        )
        for h in range(4):
            both = dot_nt(rows, gates[h])
            one = share[:, (h // 2) * HD : (h // 2 + 1) * HD]
            scale = jnp.concatenate([one, one], axis=1)[:, 0:width]
            act[:, h * width : (h + 1) * width] = (
                jnp.maximum(both[:, 0:width], 0.0) * both[:, width : 2 * width] * scale
            ).astype(jnp.bfloat16)
        for c in range(model // cols):
            at = slice(c * cols, (c + 1) * cols)
            block = jnp.dot(
                act[...],
                downs[:, :, at].reshape(4 * width, cols),
                preferred_element_type=jnp.float32,
            )
            parts[place, :, :, at] = block.astype(jnp.bfloat16).reshape(2, own, cols)
        req_copy(parts.at[place, 1 - column_of], part_in.at[place], 6, place, twin).start()

    def send_back(place):
        req_copy(part_in.at[place], part_in.at[place], 6, place, twin).wait_recv()
        parts[place, column_of] = (
            parts[place, column_of].astype(jnp.float32) + part_in[place].astype(jnp.float32)
        ).astype(jnp.bfloat16)
        req_copy(
            parts.at[place, column_of], sum_in.at[line], 7, place, along(place), line
        ).start()

    def expert_step(t, carry):
        pass_on(t + 2)
        place, _, valid = schedule(t)

        @pl.when(valid)
        def _():
            expert_rows(place)

        past, _, was_valid = schedule(lax.rem(t + 2 * steps - 2, 2 * steps))

        @pl.when((t >= 2) & was_valid)
        def _():
            send_back(past)

        return carry

    lax.fori_loop(0, 2 * steps, expert_step, 0)

    req_copy(part_in.at[line], part_in.at[line], 6, line, twin).wait_recv()
    total = (
        mid[...].astype(jnp.float32)
        + parts[line, column_of].astype(jnp.float32)
        + part_in[line].astype(jnp.float32)
    )
    for d in range(1, steps):
        place = lax.rem(line + d, steps)
        req_copy(sum_in.at[place], sum_in.at[place], 7, place, twin).wait_recv()
        total = total + sum_in[place].astype(jnp.float32)
    layer_out[...] = total.astype(jnp.bfloat16)

    for n in range(12):
        src, part, which = cached[n % 4]
        hid_copy(src, kv.at[me * 2 + part, which], n, pair).wait_send()
    for n in range(12, 18):
        hid_copy(span_rows(0, me), span_rows(0, me), n, pair).wait_send()
    for n in range(18, 24):
        ref = (gates, downs)[n % 2]
        hid_copy(ref.at[own_slot], ref.at[own_slot], n, pair).wait_send()
    for place in range(steps):
        for n in range(2):
            toks_copy(n, place, 0, twin, place).wait_send()

            @pl.when((place <= line) & (line + 1 < steps))
            def _():
                toks_copy(n, place, 1, twin, place).wait_send()

            @pl.when((place >= line) & (line >= 1))
            def _():
                toks_copy(n, place, 2, twin, place).wait_send()

        req_copy(part_in.at[place], part_in.at[place], 6, place, twin).wait_send()

        @pl.when(place != line)
        def _():
            req_copy(part_in.at[place], part_in.at[place], 7, place, twin).wait_send()


def body(
    hidden_in,
    queries,
    cache_keys,
    cache_values,
    lengths,
    routes,
    attn_gain,
    key_proj,
    value_proj,
    out_proj,
    moe_gain,
    router,
    gate_up,
    down_proj,
):
    own, model = hidden_in.shape[1:]
    kv_width = key_proj.shape[1]
    cached = cache_keys.shape[1]
    steps = lax.axis_size("req") // 2
    experts = router.shape[1]
    width = gate_up.shape[3]
    bf16 = jnp.bfloat16
    vmem = pl.BlockSpec(memory_space=pltpu.VMEM)
    smem = pl.BlockSpec(memory_space=pltpu.SMEM)
    anywhere = pl.BlockSpec(memory_space=pl.ANY)
    layer_out, new_keys, new_values = pl.pallas_call(
        functools.partial(layer_kernel, steps),
        out_shape=(
            jax.ShapeDtypeStruct((own, model), bf16),
            jax.ShapeDtypeStruct((own, kv_width), bf16),
            jax.ShapeDtypeStruct((own, kv_width), bf16),
        ),
        in_specs=[
            vmem,
            vmem,
            anywhere,
            anywhere,
            smem,
            vmem,
            vmem,
            vmem,
            vmem,
            anywhere,
            vmem,
            vmem,
            anywhere,
            anywhere,
        ],
        out_specs=(vmem, vmem, vmem),
        scratch_shapes=[
            pltpu.VMEM((9, 2, cached // 2, kv_width), bf16),
            pltpu.VMEM((KVH, GROUP * own, HD), bf16),
            pltpu.VMEM((KVH, GROUP * own, 2 * HD), jnp.float32),
            pltpu.VMEM((KVH, GROUP * own, HD), jnp.float32),
            pltpu.VMEM((own, QH * HD), bf16),
            pltpu.VMEM(out_proj.shape, bf16),
            pltpu.VMEM((own, model), bf16),
            pltpu.VMEM((4, 2 * width, model), bf16),
            pltpu.VMEM((4, width, model), bf16),
            pltpu.VMEM((2 * own, 4 * width), bf16),
            pltpu.VMEM((steps, 2, own, model), bf16),
            pltpu.VMEM((steps, 2, 2 * experts, own), bf16),
            pltpu.VMEM((steps, 2, own, model), bf16),
            pltpu.VMEM((steps, own, model), bf16),
            pltpu.VMEM((steps, own, model), bf16),
            pltpu.SemaphoreType.DMA((7,)),
            pltpu.SemaphoreType.DMA((24,)),
            pltpu.SemaphoreType.DMA((24,)),
            pltpu.SemaphoreType.DMA((8, steps)),
            pltpu.SemaphoreType.DMA((8, steps)),
        ],
        compiler_params=pltpu.CompilerParams(
            collective_id=0, has_side_effects=True, vmem_limit_bytes=VMEM_LIMIT
        ),
    )(
        hidden_in[0],
        queries[0],
        cache_keys[0],
        cache_values[0],
        lengths,
        routes[0].T,
        attn_gain,
        key_proj,
        value_proj,
        out_proj,
        moe_gain,
        router.T,
        jnp.swapaxes(gate_up[0], 1, 2).reshape(2 * width, model),
        down_proj[0],
    )
    return (layer_out[None], new_keys[None], new_values[None])


VMEM_LIMIT = 64 * 1024 * 1024 - 512 * 1024


def solution(mesh):
    in_specs = (
        P("req", "hid", None),
        P("req", "hid", None),
        P("req", "hid", None),
        P("req", "hid", None),
        P("req"),
        P("req", None, None),
        P(),
        P(),
        P(),
        P(),
        P(),
        P(),
        P("req", None, None, "hid"),
        P("req", "hid", None),
    )
    out_specs = (P("req", "hid", None), P("req", "hid", None), P("req", "hid", None))
    return jax.shard_map(body, mesh=mesh, in_specs=in_specs, out_specs=out_specs, check_vma=False)
```

```python
import functools

import jax
import jax.numpy as jnp
from jax import lax
from jax.experimental import pallas as pl
from jax.experimental.pallas import tpu as pltpu
from jax.sharding import PartitionSpec as P

QH = 12
KVH = 2
HD = 128
GROUP = QH // KVH
EPS = 1e-06
MASKED_SCORE = -1e30
EXP2_SCALE = HD ** (-0.5) * 1.4426950408889634
ROW_TILE = 256
MESH = pl.DeviceIdType.MESH


def normalize(row_data, gain_vector):
    row_data = row_data.astype(jnp.float32)
    return (
        row_data
        * lax.rsqrt(jnp.mean(row_data * row_data, axis=-1, keepdims=True) + EPS)
        * gain_vector
    )


def dot_nt(left, right):
    return lax.dot_general(
        left, right, (((1,), (1,)), ((), ())), preferred_element_type=jnp.float32
    )


def layer_kernel(
    steps,
    hidden,
    queries,
    cache_keys,
    cache_values,
    lengths,
    routes_t,
    attn_gain,
    key_proj,
    value_proj,
    out_proj,
    moe_gain,
    router_t,
    gate_up,
    down_proj,
    layer_out,
    new_keys,
    new_values,
    kv,
    heads,
    acc,
    row_max,
    attended,
    out_w,
    mid,
    gates,
    downs,
    act,
    toks,
    wts,
    parts,
    part_in,
    sum_in,
    local_sem,
    hid_send,
    hid_recv,
    req_send,
    req_recv,
):
    own = hidden.shape[0]
    half = cache_keys.shape[0] // 2
    span_slot = kv.shape[0] - 1
    width = down_proj.shape[0]
    experts = router_t.shape[0]
    me = lax.axis_index("hid")
    pair = me + 1 - 2 * lax.rem(me, 2)
    across = lax.rem(me + 2, 4)
    corner = 3 - me
    row = lax.axis_index("req")
    line, side = row // 2, lax.rem(row, 2)
    core, column_of = lax.rem(me, 2), me // 2
    own_slot, pair_slot = side * 2 + core, side * 2 + 1 - core
    far_slot, corner_slot = (1 - side) * 2 + core, (1 - side) * 2 + 1 - core
    neighbour = {"req": line * 2 + 1 - side}
    twin = {"hid": across}

    def along(place):
        return {"req": place * 2 + side}

    barrier = pltpu.get_barrier_semaphore()
    others = [along(lax.rem(line + d, steps)) for d in range(1, steps)]
    for peer in [{"hid": pair}, twin, neighbour] + others:
        pl.semaphore_signal(barrier, inc=1, device_id=peer, device_id_type=MESH)
    pl.semaphore_wait(barrier, steps + 2)

    def hid_copy(src, dst, number, peer):
        peer = peer if isinstance(peer, dict) else {"hid": peer}
        return pltpu.make_async_remote_copy(
            src_ref=src,
            dst_ref=dst,
            send_sem=hid_send.at[number],
            recv_sem=hid_recv.at[number],
            device_id=peer,
            device_id_type=MESH,
        )

    def req_copy(src, dst, kind, slot, peer, landing=None):
        return pltpu.make_async_remote_copy(
            src_ref=src,
            dst_ref=dst,
            send_sem=req_send.at[kind, slot],
            recv_sem=req_recv.at[kind, slot if landing is None else landing],
            device_id=peer,
            device_id_type=MESH,
        )

    cached = [
        (ref.at[pl.ds(part * half, half)], part, which)
        for part in range(2)
        for which, ref in enumerate((cache_keys, cache_values))
    ]
    for n, (src, part, which) in enumerate(cached[:2]):
        hid_copy(src, kv.at[me * 2 + part, which], n, across).start()
    for n, (src, part, which) in enumerate(cached):
        hid_copy(src, kv.at[me * 2 + part, which], 4 + n, pair).start()

    def own_block(n):
        src, part, which = cached[n]
        return pltpu.make_async_copy(src, kv.at[me * 2 + part, which], local_sem.at[n])

    for n in range(4):
        own_block(n).start()
    for n, peer in ((18, neighbour), (20, pair)):
        hid_copy(gate_up, gates.at[own_slot], n, peer).start()
        hid_copy(down_proj, downs.at[own_slot], n + 1, peer).start()
    gate_load = pltpu.make_async_copy(gate_up, gates.at[own_slot], local_sem.at[4])
    gate_load.start()
    down_load = pltpu.make_async_copy(down_proj, downs.at[own_slot], local_sem.at[5])
    down_load.start()
    out_load = pltpu.make_async_copy(out_proj, out_w, local_sem.at[6])
    out_load.start()

    normed = normalize(hidden[...], attn_gain[...]).astype(jnp.bfloat16)
    own_rows = pl.ds(pl.multiple_of(me * own, own), own)
    for which, (proj, dest) in enumerate(((key_proj, new_keys), (value_proj, new_values))):
        fresh = jnp.dot(normed, proj[...], preferred_element_type=jnp.float32).astype(jnp.bfloat16)
        dest[...] = fresh
        kv[span_slot, which, own_rows, :] = fresh

    def span_rows(which, owner):
        return kv.at[span_slot, which, pl.ds(pl.multiple_of(owner * own, own), own)]

    for which in range(2):
        hid_copy(span_rows(which, me), span_rows(which, me), 12 + which, across).start()
        hid_copy(span_rows(which, me), span_rows(which, me), 14 + which, pair).start()
    for n, (src, part, which) in enumerate(cached[2:]):
        hid_copy(src, kv.at[me * 2 + part, which], 2 + n, across).start()

    for g in range(KVH):
        for i in range(GROUP):
            heads[g, i * own : (i + 1) * own, :] = queries[
                :, (g * GROUP + i) * HD : (g * GROUP + i + 1) * HD
            ]
    acc[...] = jnp.zeros_like(acc)
    row_max[...] = jnp.full_like(row_max, MASKED_SCORE)

    def landed(dst, number):
        hid_copy(dst, dst, number, pair).wait_recv()

    length = lengths[0]

    def absorb(slots, hide):
        for g in range(KVH):
            keys = jnp.concatenate(
                [kv[slot, 0, :, g * HD : (g + 1) * HD] for slot in slots], axis=0
            )
            values = jnp.concatenate(
                [kv[slot, 1, :, g * HD : (g + 1) * HD] for slot in slots], axis=0
            )
            values = jnp.concatenate([values, jnp.ones_like(values)], axis=1)
            for tile in range(GROUP * own // ROW_TILE):
                rows = slice(tile * ROW_TILE, (tile + 1) * ROW_TILE)
                scores = hide(dot_nt(heads[g, rows, :], keys))
                old_max = row_max[g, rows, :]
                new_max = jnp.maximum(old_max, jnp.max(scores, axis=1, keepdims=True))
                row_max[g, rows, :] = new_max
                rescale = jnp.exp2((old_max - new_max) * EXP2_SCALE)
                shift = jnp.concatenate([new_max] * (len(slots) * half // HD), axis=1)
                probs = jnp.exp2((scores - shift) * EXP2_SCALE).astype(jnp.bfloat16)
                acc[g, rows, :] = acc[g, rows, :] * jnp.concatenate([rescale, rescale], axis=1) + (
                    jnp.dot(probs, values, preferred_element_type=jnp.float32)
                )

    def step_body(step, carry):
        for n in range(2):

            @pl.when(step == 0)
            def _():
                own_block(2 * n).wait()
                own_block(2 * n + 1).wait()

            @pl.when(step == 1)
            def _():
                for which in range(2):
                    landed(kv.at[pair * 2 + n, which], 4 + 2 * n + which)

            @pl.when(step == 2 + 2 * n)
            def _():
                for which in range(2):
                    block = kv.at[across * 2 + n, which]
                    landed(block, 2 * n + which)
                    hid_copy(block, block, 8 + 2 * n + which, pair).start()

                for which in range(2):
                    landed(kv.at[corner * 2 + n, which], 8 + 2 * n + which)

        @pl.when(step == 3)
        def _():
            for which in range(2):
                block = span_rows(which, across)
                landed(block, 12 + which)
                hid_copy(block, block, 16 + which, pair).start()
            for which in range(2):
                landed(span_rows(which, pair), 14 + which)
                landed(span_rows(which, corner), 16 + which)

        late = (step + 2) // 4
        early = 1 - late
        part = step // 4
        source = me + lax.rem(step, 2) * (pair - me)
        first = early * 2 * source + late * (2 * across + part)
        second = early * (2 * source + 1) + late * (2 * corner + part)

        @pl.when(step != 3)
        def _():
            column = lax.broadcasted_iota(jnp.int32, (1, half), 1)
            bias = jnp.concatenate(
                [
                    jnp.where(column < length - slot * half, 0.0, MASKED_SCORE)
                    for slot in (first, second)
                ],
                axis=1,
            )
            absorb((first, second), lambda scores: scores + bias)

        @pl.when(step == 3)
        def _():
            token = lax.broadcasted_iota(jnp.int32, (ROW_TILE, half), 0) % own
            column = lax.broadcasted_iota(jnp.int32, (ROW_TILE, half), 1)
            visible = column <= me * own + token
            absorb((span_slot,), lambda scores: jnp.where(visible, scores, MASKED_SCORE))

        return carry

    lax.fori_loop(0, 5, step_body, 0)

    for g in range(KVH):
        for i in range(GROUP):
            rows = slice(i * own, (i + 1) * own)
            head = g * GROUP + i
            attended[:, head * HD : (head + 1) * HD] = (
                acc[g, rows, 0:HD] / acc[g, rows, HD : 2 * HD]
            ).astype(jnp.bfloat16)
    out_load.wait()
    cols = 512
    model = hidden.shape[1]
    for c in range(model // cols):
        at = slice(c * cols, (c + 1) * cols)
        mid[:, at] = (
            hidden[:, at].astype(jnp.float32)
            + jnp.dot(attended[...], out_w[:, at], preferred_element_type=jnp.float32)
        ).astype(jnp.bfloat16)

    moe_in = normalize(mid[...], moe_gain[...]).astype(jnp.bfloat16)
    toks[line, column_of] = moe_in
    logits = dot_nt(router_t[...], moe_in)
    own_routes = routes_t[:, own_rows]
    expert_ids = lax.broadcasted_iota(jnp.int32, (experts, own), 0)
    chosen = expert_ids == own_routes[0:1, :]
    for k in range(1, own_routes.shape[0]):
        chosen = chosen | (expert_ids == own_routes[k : k + 1, :])
    gate_values = jnp.where(chosen, jax.nn.sigmoid(logits), 0.0)
    weights = gate_values / jnp.sum(gate_values, axis=0, keepdims=True)
    high = weights.astype(jnp.bfloat16).astype(jnp.float32)
    wts[line, column_of] = jnp.concatenate([high, weights - high], axis=0).astype(jnp.bfloat16)

    def toks_copy(n, place, kind, peer, slot):
        block = (toks, wts)[n].at[place, column_of]
        return req_copy(block, block, 2 * kind + n, slot, peer)

    def give(place, up, down):
        for n in range(2):

            @pl.when(up)
            def _():
                toks_copy(n, place, 1, along(line + 1), place).start()

            @pl.when(down)
            def _():
                toks_copy(n, place, 2, along(line - 1), place).start()

            toks_copy(n, place, 0, twin, place).start()

    def schedule(t):
        dist = lax.rem(t // 2 + 1, steps)
        up = lax.rem(t, 2)
        place = line - dist + 2 * dist * up
        return place, up, (place >= 0) & (place < steps) & (t < 2 * steps - 1)

    def pass_on(t):
        place, up, valid = schedule(t)
        valid = valid & (t < 2 * steps - 2)
        for n in range(2):

            @pl.when(valid & (up == 0))
            def _():
                toks_copy(n, place, 1, twin, place).wait_recv()

                @pl.when(line + 1 < steps)
                def _():
                    toks_copy(n, place, 1, along(line + 1), place).start()

            @pl.when(valid & (up == 1))
            def _():
                toks_copy(n, place, 2, twin, place).wait_recv()

                @pl.when(line >= 1)
                def _():
                    toks_copy(n, place, 2, along(line - 1), place).start()

            @pl.when(valid)
            def _():
                toks_copy(n, place, 0, twin, place).start()

    give(line, line + 1 < steps, line >= 1)

    pass_on(0)
    pass_on(1)

    gate_load.wait()
    down_load.wait()
    for n, ref in enumerate((gates, downs)):
        landed(ref.at[far_slot], 18 + n)
        hid_copy(ref.at[far_slot], ref.at[far_slot], 22 + n, pair).start()
    for n, ref in enumerate((gates, downs)):
        landed(ref.at[pair_slot], 20 + n)
        landed(ref.at[corner_slot], 22 + n)

    lane_half = lax.broadcasted_iota(jnp.int32, (2 * experts, 2 * HD), 1) // HD
    pick = (
        lax.broadcasted_iota(jnp.int32, (2 * experts, 2 * HD), 0) % experts == line * 2 + lane_half
    ).astype(jnp.bfloat16)

    def expert_rows(place):
        for n, ref in enumerate((toks, wts)):
            block = ref.at[place, 1 - column_of]
            req_copy(block, block, n, place, twin).wait_recv()
        rows = toks[place].reshape(2 * own, model)
        share = jnp.concatenate(
            [
                lax.dot_general(
                    wts[place, s],
                    pick,
                    (((0,), (0,)), ((), ())),
                    preferred_element_type=jnp.float32,
                )
                for s in range(2)
            ],
            axis=0,
        )
        for h in range(4):
            both = dot_nt(rows, gates[h])
            one = share[:, (h // 2) * HD : (h // 2 + 1) * HD]
            scale = jnp.concatenate([one, one], axis=1)[:, 0:width]
            act[:, h * width : (h + 1) * width] = (
                jnp.maximum(both[:, 0:width], 0.0) * both[:, width : 2 * width] * scale
            ).astype(jnp.bfloat16)
        for c in range(model // cols):
            at = slice(c * cols, (c + 1) * cols)
            block = jnp.dot(
                act[...],
                downs[:, :, at].reshape(4 * width, cols),
                preferred_element_type=jnp.float32,
            )
            parts[place, :, :, at] = block.astype(jnp.bfloat16).reshape(2, own, cols)
        req_copy(parts.at[place, 1 - column_of], part_in.at[place], 6, place, twin).start()

    def send_back(place):
        req_copy(part_in.at[place], part_in.at[place], 6, place, twin).wait_recv()
        parts[place, column_of] = (
            parts[place, column_of].astype(jnp.float32) + part_in[place].astype(jnp.float32)
        ).astype(jnp.bfloat16)
        req_copy(
            parts.at[place, column_of], sum_in.at[line], 7, place, along(place), line
        ).start()

    def expert_step(t, carry):
        pass_on(t + 2)
        place, _, valid = schedule(t)

        @pl.when(valid)
        def _():
            expert_rows(place)

        past, _, was_valid = schedule(lax.rem(t + 2 * steps - 2, 2 * steps))

        @pl.when((t >= 2) & was_valid)
        def _():
            send_back(past)

        return carry

    lax.fori_loop(0, 2 * steps, expert_step, 0)

    req_copy(part_in.at[line], part_in.at[line], 6, line, twin).wait_recv()
    total = (
        mid[...].astype(jnp.float32)
        + parts[line, column_of].astype(jnp.float32)
        + part_in[line].astype(jnp.float32)
    )
    for d in range(1, steps):
        place = lax.rem(line + d, steps)
        req_copy(sum_in.at[place], sum_in.at[place], 7, place, twin).wait_recv()
        total = total + sum_in[place].astype(jnp.float32)
    layer_out[...] = total.astype(jnp.bfloat16)

    for n in range(12):
        src, part, which = cached[n % 4]
        hid_copy(src, kv.at[me * 2 + part, which], n, pair).wait_send()
    for n in range(12, 18):
        hid_copy(span_rows(0, me), span_rows(0, me), n, pair).wait_send()
    for n in range(18, 24):
        ref = (gates, downs)[n % 2]
        hid_copy(ref.at[own_slot], ref.at[own_slot], n, pair).wait_send()
    for place in range(steps):
        for n in range(2):
            toks_copy(n, place, 0, twin, place).wait_send()

            @pl.when((place <= line) & (line + 1 < steps))
            def _():
                toks_copy(n, place, 1, twin, place).wait_send()

            @pl.when((place >= line) & (line >= 1))
            def _():
                toks_copy(n, place, 2, twin, place).wait_send()

        req_copy(part_in.at[place], part_in.at[place], 6, place, twin).wait_send()

        @pl.when(place != line)
        def _():
            req_copy(part_in.at[place], part_in.at[place], 7, place, twin).wait_send()


def body(
    hidden_in,
    queries,
    cache_keys,
    cache_values,
    lengths,
    routes,
    attn_gain,
    key_proj,
    value_proj,
    out_proj,
    moe_gain,
    router,
    gate_up,
    down_proj,
):
    own, model = hidden_in.shape[1:]
    kv_width = key_proj.shape[1]
    cached = cache_keys.shape[1]
    steps = lax.axis_size("req") // 2
    experts = router.shape[1]
    width = gate_up.shape[3]
    bf16 = jnp.bfloat16
    vmem = pl.BlockSpec(memory_space=pltpu.VMEM)
    smem = pl.BlockSpec(memory_space=pltpu.SMEM)
    anywhere = pl.BlockSpec(memory_space=pl.ANY)
    layer_out, new_keys, new_values = pl.pallas_call(
        functools.partial(layer_kernel, steps),
        out_shape=(
            jax.ShapeDtypeStruct((own, model), bf16),
            jax.ShapeDtypeStruct((own, kv_width), bf16),
            jax.ShapeDtypeStruct((own, kv_width), bf16),
        ),
        in_specs=[
            vmem,
            vmem,
            anywhere,
            anywhere,
            smem,
            vmem,
            vmem,
            vmem,
            vmem,
            anywhere,
            vmem,
            vmem,
            anywhere,
            anywhere,
        ],
        out_specs=(vmem, vmem, vmem),
        scratch_shapes=[
            pltpu.VMEM((9, 2, cached // 2, kv_width), bf16),
            pltpu.VMEM((KVH, GROUP * own, HD), bf16),
            pltpu.VMEM((KVH, GROUP * own, 2 * HD), jnp.float32),
            pltpu.VMEM((KVH, GROUP * own, HD), jnp.float32),
            pltpu.VMEM((own, QH * HD), bf16),
            pltpu.VMEM(out_proj.shape, bf16),
            pltpu.VMEM((own, model), bf16),
            pltpu.VMEM((4, 2 * width, model), bf16),
            pltpu.VMEM((4, width, model), bf16),
            pltpu.VMEM((2 * own, 4 * width), bf16),
            pltpu.VMEM((steps, 2, own, model), bf16),
            pltpu.VMEM((steps, 2, 2 * experts, own), bf16),
            pltpu.VMEM((steps, 2, own, model), bf16),
            pltpu.VMEM((steps, own, model), bf16),
            pltpu.VMEM((steps, own, model), bf16),
            pltpu.SemaphoreType.DMA((7,)),
            pltpu.SemaphoreType.DMA((24,)),
            pltpu.SemaphoreType.DMA((24,)),
            pltpu.SemaphoreType.DMA((8, steps)),
            pltpu.SemaphoreType.DMA((8, steps)),
        ],
        compiler_params=pltpu.CompilerParams(
            collective_id=0, has_side_effects=True, vmem_limit_bytes=VMEM_LIMIT
        ),
    )(
        hidden_in[0],
        queries[0],
        cache_keys[0],
        cache_values[0],
        lengths,
        routes[0].T,
        attn_gain,
        key_proj,
        value_proj,
        out_proj,
        moe_gain,
        router.T,
        jnp.swapaxes(gate_up[0], 1, 2).reshape(2 * width, model),
        down_proj[0],
    )
    return (layer_out[None], new_keys[None], new_values[None])


VMEM_LIMIT = 64 * 1024 * 1024 - 512 * 1024


def solution(mesh):
    in_specs = (
        P("req", "hid", None),
        P("req", "hid", None),
        P("req", "hid", None),
        P("req", "hid", None),
        P("req"),
        P("req", None, None),
        P(),
        P(),
        P(),
        P(),
        P(),
        P(),
        P("req", None, None, "hid"),
        P("req", "hid", None),
    )
    out_specs = (P("req", "hid", None), P("req", "hid", None), P("req", "hid", None))
    return jax.shard_map(body, mesh=mesh, in_specs=in_specs, out_specs=out_specs, check_vma=False)
```
